32 devices in a mesh: rep: 2 (over x), led: 16 (over z, y, core).
Axes of the slice: x: 2, y: 2, z: 4, core: 2. Of those that a mesh axis runs over, the one named last changes fastest.
Arguments:
- spectrum: bfloat16 [96, 16, 2, 6144], P(('rep', 'led')), parts along dimension 0, may hold values from -6 to 6
- block_owner: int32 [24], replicated, may hold values from 0 to 15, as said below
- row_offset: int32 [16], replicated, may hold values from 0 to 128
- column_offset: int32 [16], replicated, may hold values from 0 to 5888
- pupil_modes: bfloat16 [8, 2, 256, 256], replicated, may hold values from -6 to 6
- amplitude: float32 [32, 512, 512], P(('rep', 'led')), parts along dimension 0, may hold values from 1 to 4
Outputs:
- spectrum_grad: float32 [96, 16, 2, 6144], P(('rep', 'led')), parts along dimension 0
The draws below stay inside these ranges and needn't reach their ends.
There are 2 independent parts, one for each index of `rep`. The reference program is written for one: setup_inputs(seed, part) draws one part's arguments, and reference() takes and returns one part's arrays. A program takes and returns all parts, laid end to end along the dimension named above; an argument that names none is the same for every part. Nothing has to cross between parts.
Inputs may be any that keep to these rules, and one draw needn't show every extreme that they name: `block_owner`: every device owns 1 to 3 blocks and some device owns exactly 3; a device's blocks fill its first slots in increasing block order, and no output reads its remaining slots.
All inputs are finite; a program needn't handle non-finite values.
Results may differ from the reference program's by a relative error of at most 0.0095.
Values may be sent and summed in bfloat16 or wider, within the bound.
A program may use at most 128 MiB of HBM per device.

```python
import math
import jax
import jax.numpy as jnp
from jax import lax

M = 512
K = 256
MODES = 8
COLS = 6144
ROWS = 384
SLOTS = 3
NBLK = 24
BLK = 16
N_LED = 16


def draw_block_owner(key, part):
    key = jax.random.fold_in(key, 11)
    first_key, second_key = jax.random.split(key)
    order = jax.random.permutation(first_key, N_LED).astype(jnp.int32)
    position = jnp.arange(N_LED, dtype=jnp.int32)
    count_at = 1 + (position < N_LED // 8 + N_LED // 4).astype(jnp.int32) + (position < N_LED // 8).astype(jnp.int32)
    counts = jnp.zeros((N_LED,), jnp.int32).at[order].set(count_at)
    slot_index = jnp.arange(N_LED * SLOTS, dtype=jnp.int32)
    device_of = slot_index // SLOTS
    used = slot_index % SLOTS < counts[device_of]
    ranked = jnp.argsort(jnp.where(used, 0, 1).astype(jnp.int32), stable=True)
    owners = device_of[ranked[:NBLK]]
    return jax.random.permutation(second_key, owners).astype(jnp.int32)


def plant(array, key, low, top_value):
    longest = array.shape.index(max(array.shape))
    spots = []
    for shift in (0, 1):
        where = [jax.random.randint(jax.random.fold_in(key, axis), (), 0, length) for axis, length in enumerate(array.shape)]
        where[longest] = (where[longest] + shift) % array.shape[longest]
        spots.append(tuple(where))
    return array.at[spots[0]].set(low).at[spots[1]].set(top_value)


def level_of(stream_key, shape, cuts, smallest, largest):
    loudness = 1.0
    for axis_at, shards_of in cuts:
        draws = jax.random.uniform(jax.random.fold_in(jax.random.fold_in(stream_key, 6), axis_at), (shards_of,), jnp.float32, smallest / len(cuts), largest / len(cuts))
        loudness = loudness * jnp.repeat(jnp.exp(draws), shape[axis_at] // shards_of).reshape((-1,) + (1,) * (len(shape) - 1 - axis_at))
    return loudness


def centred(own_key, shape, spread, most, shards=(), kind=jnp.bfloat16):
    entries = spread * jax.random.normal(own_key, shape, jnp.float32)
    if shards:
        entries = entries * level_of(own_key, shape, shards, -0.22, 0.18)
    return jnp.clip(entries, -most, most).astype(kind)


def setup_inputs(seed: int = 0, part: int = 0) -> dict:
    seeds = jax.random.split(jax.random.key(seed), 7)
    part_keys = jax.random.split(jax.random.fold_in(seeds[6], part), 7)
    spectrum = centred(part_keys[0], (N_LED * SLOTS, BLK, 2, COLS), 1.0, 6.0, ((0, 16),))
    block_owner = draw_block_owner(jax.random.fold_in(seeds[6], 71), part)
    row_offset = plant(jax.random.randint(seeds[2], (N_LED,), 0, ROWS - K + 1), jax.random.fold_in(seeds[2], 1), 0, ROWS - K).astype(jnp.int32)
    column_offset = plant(jax.random.randint(seeds[3], (N_LED,), 0, COLS - K + 1), jax.random.fold_in(seeds[3], 1), 0, COLS - K).astype(jnp.int32)
    pupil_modes = centred(seeds[4], (MODES, 2, K, K), 1.0, 6.0)
    amplitude = jnp.clip(1.0 + 3.0 * jax.random.uniform(part_keys[5], (N_LED, M, M), jnp.float32) ** level_of(part_keys[5], (N_LED, M, M), ((0, 16),), -0.2, 0.2), 1.0, 4.0)
    return dict(spectrum=spectrum, block_owner=block_owner, row_offset=row_offset, column_offset=column_offset, pupil_modes=pupil_modes, amplitude=amplitude)


amp_eps = 0.1

def slot_map(block_owner, slot_count):
    order = jnp.arange(block_owner.shape[0], dtype=jnp.int32)
    same_before = (block_owner[None, :] == block_owner[:, None]) & (order[None, :] < order[:, None])
    rank_in_owner = lax.optimization_barrier(jnp.sum(same_before.astype(jnp.int32), axis=1))
    return (block_owner * slot_count + rank_in_owner).astype(jnp.int32)

def dft_tables(image_side, window_side):
    pixel = jnp.arange(image_side, dtype=jnp.int32)[:, None]
    freq = jnp.arange(window_side, dtype=jnp.int32)[None, :] - window_side // 2
    phase = jnp.mod(pixel * freq, image_side).astype(jnp.float32) * (2.0 * math.pi / image_side)
    scale = 1.0 / math.sqrt(image_side)
    real_part = (jnp.cos(phase) * scale).astype(jnp.bfloat16)
    imag_part = (jnp.sin(phase) * scale).astype(jnp.bfloat16)
    left_table = jnp.stack([jnp.stack([real_part, -imag_part]), jnp.stack([imag_part, real_part])])
    right_table = jnp.stack([jnp.stack([real_part.T, imag_part.T]), jnp.stack([-imag_part.T, real_part.T])])
    return (left_table, right_table)

def mode_gradient(window, pupil_modes, image_amp, left_table, right_table):
    spec_real = window[0].astype(jnp.float32)
    spec_imag = window[1].astype(jnp.float32)
    pupil_real = pupil_modes[:, 0].astype(jnp.float32)
    pupil_imag = pupil_modes[:, 1].astype(jnp.float32)
    pupil_field = jnp.stack([spec_real * pupil_real - spec_imag * pupil_imag, spec_real * pupil_imag + spec_imag * pupil_real], axis=1).astype(jnp.bfloat16)
    hp = lax.Precision.HIGHEST
    half_transform = jnp.einsum('kcuv,cdvq->kduq', pupil_field.astype(jnp.float32), right_table.astype(jnp.float32), precision=hp).astype(jnp.bfloat16)
    image_field = jnp.einsum('edpu,kduq->kepq', left_table.astype(jnp.float32), half_transform.astype(jnp.float32), precision=hp)
    intensity = lax.optimization_barrier(jnp.sum(image_field * image_field, axis=(0, 1)))
    modulus = jnp.sqrt(intensity + amp_eps)
    weight = (modulus - image_amp) / modulus
    field_grad = (image_field * weight[None, None]).astype(jnp.bfloat16)
    back_half = jnp.einsum('deup,kepq->kduq', right_table.astype(jnp.float32), field_grad.astype(jnp.float32), precision=hp).astype(jnp.bfloat16)
    window_grad = jnp.einsum('kduq,dcqv->kcuv', back_half.astype(jnp.float32), left_table.astype(jnp.float32), precision=hp)
    grad_real = lax.optimization_barrier(jnp.sum(pupil_real * window_grad[:, 0] + pupil_imag * window_grad[:, 1], axis=0))
    grad_imag = lax.optimization_barrier(jnp.sum(pupil_real * window_grad[:, 1] - pupil_imag * window_grad[:, 0], axis=0))
    return jnp.stack([grad_real, grad_imag])

def reference(spectrum, block_owner, row_offset, column_offset, pupil_modes, amplitude):
    slot_of_block = slot_map(block_owner, SLOTS)
    blocks = spectrum[slot_of_block]
    spectrum_band = blocks.reshape(ROWS, 2, COLS)
    left_table, right_table = dft_tables(M, K)

    def one_led(grad_band, led_index):
        row_start = row_offset[led_index].astype(jnp.int32)
        col_start = column_offset[led_index].astype(jnp.int32)
        zero_index = jnp.int32(0)
        window = lax.dynamic_slice(spectrum_band, (row_start, zero_index, col_start), (K, 2, K))
        window = jnp.transpose(window, (1, 0, 2))
        led_grad = mode_gradient(window, pupil_modes, amplitude[led_index], left_table, right_table)
        led_grad = jnp.transpose(led_grad, (1, 0, 2))
        current = lax.dynamic_slice(grad_band, (row_start, zero_index, col_start), (K, 2, K))
        grad_band = lax.dynamic_update_slice(grad_band, current + led_grad, (row_start, zero_index, col_start))
        return (grad_band, None)
    start_band = jnp.zeros((ROWS, 2, COLS), jnp.float32)
    grad_band = lax.scan(one_led, start_band, jnp.arange(N_LED, dtype=jnp.int32))[0]
    gradient_slots = jnp.zeros((N_LED * SLOTS, BLK, 2, COLS), jnp.float32)
    return gradient_slots.at[slot_of_block].set(grad_band.reshape(NBLK, BLK, 2, COLS))
```

```python
import functools
import math

import jax
import jax.numpy as jnp
import ml_dtypes
import numpy as np
from jax import lax
from jax.experimental import pallas as pl
from jax.experimental.pallas import tpu as pltpu
from jax.sharding import PartitionSpec as P

amp_eps = 0.1
f32 = jnp.float32
bf16 = jnp.bfloat16
VMEM = pl.BlockSpec(memory_space=pltpu.VMEM)
SMEM = pl.BlockSpec(memory_space=pltpu.SMEM)


def dft_tables(image_side, window_side):
    half = image_side // 2
    pixel = np.arange(half, dtype=np.int64)[:, None]
    freq = np.arange(window_side, dtype=np.int64)[None, :] - window_side // 2
    phase = np.mod(pixel * freq, image_side).astype(np.float64) * (2.0 * math.pi / image_side)
    scale = 1.0 / math.sqrt(image_side)
    real = (np.cos(phase) * scale).astype(np.float32).astype(ml_dtypes.bfloat16)
    imag = (np.sin(phase) * scale).astype(np.float32).astype(ml_dtypes.bfloat16)
    left = []
    for parity in (0, 1):
        a, b = real[:, parity::2], imag[:, parity::2]
        left.append(np.block([[a, -b], [b, a]]))
    left = np.stack(left)
    right = np.ascontiguousarray(left.transpose(0, 2, 1))
    return left, right


def deinterleave(side):
    order = np.concatenate([np.arange(0, side, 2), np.arange(1, side, 2)])
    perm = (np.arange(side)[:, None] == order[None, :]).astype(ml_dtypes.bfloat16)
    return perm, np.ascontiguousarray(perm.T)


def dot(a, b):
    return jnp.dot(a, b, preferred_element_type=f32)


def aligned(column, span, columns):
    base = jnp.minimum((column // 128) * 128, columns - span)
    return pl.multiple_of(base, 128), column - base


def crop_kernel(column_ref, spectrum_ref, out_ref):
    led_count, slots, _, double = out_ref.shape
    window = double // 2
    columns = spectrum_ref.shape[3]
    span = window + 128

    @pl.loop(0, led_count)
    def _(led):
        base, shift = aligned(column_ref[led], span, columns)
        for s in range(slots):
            for c in range(2):
                wide = spectrum_ref[c, s, :, pl.ds(base, span)].astype(f32)
                wide = pltpu.roll(wide, span - shift, 1)
                out_ref[led, s, :, c * window:(c + 1) * window] = wide[:, :window].astype(bf16)


def gradient_kernel(
    owner_ref, row_ref, strips_ref, pupil_ref, amp_ref, left_ref, right_ref, perm_ref, out_ref,
    band, psi, pupil, weight, total, used, place,
):
    led_count, slots, blk, double = strips_ref.shape
    modes, _, w, _ = pupil_ref.shape
    m = amp_ref.shape[1]
    half, h = m // 2, w // 2
    block_count = owner_ref.shape[0]
    rows = block_count * blk
    my_row = row_ref[lax.axis_index("led")]

    for n in range(led_count):
        used[n] = 0
    for b in range(block_count):
        owner = owner_ref[b]
        rank = used[owner]
        used[owner] = rank + 1
        place[b] = rank
        band[b * blk:(b + 1) * blk, :] = strips_ref[owner, rank].astype(f32)

    line = lax.broadcasted_iota(jnp.int32, (w, rows), 0)
    natural = jnp.where(line < h, 2 * line, 2 * line - w + 1)
    chosen = lax.broadcasted_iota(jnp.int32, (w, rows), 1) == natural + my_row
    chosen = jnp.where(chosen, 1.0, 0.0).astype(bf16)
    spread, gather = perm_ref[0], perm_ref[1]
    picked = dot(chosen, band[...].astype(bf16)).astype(bf16)
    xr = dot(picked[:, :w], spread)
    xi = dot(picked[:, w:], spread)

    weight[...] = jnp.zeros_like(weight)

    @pl.loop(0, modes)
    def _(k):
        parts = []
        for c in range(2):
            mixed = dot(gather, pupil_ref[k, c]).astype(bf16)
            mixed = dot(mixed, spread)
            pupil[k, c] = mixed.astype(bf16)
            parts.append(mixed)
        pr, pi = parts
        yr = (xr * pr - xi * pi).astype(bf16)
        yi = (xr * pi + xi * pr).astype(bf16)
        even = dot(jnp.concatenate([yr[:, :h], yi[:, :h]], 1), right_ref[0])
        odd = dot(jnp.concatenate([yr[:, h:], yi[:, h:]], 1), right_ref[1])
        low = (even + odd).astype(bf16)
        high = (even - odd).astype(bf16)

        def stacked(lo, hi):
            return jnp.concatenate(
                [
                    jnp.concatenate([low[lo:hi, :half], high[lo:hi, :half]], 1),
                    jnp.concatenate([low[lo:hi, half:], high[lo:hi, half:]], 1),
                ],
                0,
            )

        even = dot(left_ref[0], stacked(0, h))
        odd = dot(left_ref[1], stacked(h, w))
        top = even + odd
        bottom = even - odd
        psi[k, 0] = top
        psi[k, 1] = bottom
        weight[:half] += top[:half] * top[:half] + top[half:] * top[half:]
        weight[half:] += bottom[:half] * bottom[:half] + bottom[half:] * bottom[half:]

    modulus = jnp.sqrt(weight[...] + amp_eps)
    weight[...] = (modulus - amp_ref[0]) / modulus
    total[...] = jnp.zeros_like(total)

    @pl.loop(0, modes)
    def _(k):
        wt = weight[:half]
        wb = weight[half:]
        sums, differences = [], []
        for part in (slice(0, half), slice(half, m)):
            top = psi[k, 0, part] * wt
            bottom = psi[k, 1, part] * wb
            sums.append((top + bottom).astype(bf16))
            differences.append((top - bottom).astype(bf16))
        even = dot(right_ref[0], jnp.concatenate(sums, 0))
        odd = dot(right_ref[1], jnp.concatenate(differences, 0))
        hr = jnp.concatenate([even[:h], odd[:h]], 0)
        hi = jnp.concatenate([even[h:], odd[h:]], 0)
        plus = jnp.concatenate([hr[:, :half] + hr[:, half:], hi[:, :half] + hi[:, half:]], 1)
        minus = jnp.concatenate([hr[:, :half] - hr[:, half:], hi[:, :half] - hi[:, half:]], 1)
        even = dot(plus.astype(bf16), left_ref[0])
        odd = dot(minus.astype(bf16), left_ref[1])
        er = jnp.concatenate([even[:, :h], odd[:, :h]], 1)
        ei = jnp.concatenate([even[:, h:], odd[:, h:]], 1)
        pr = pupil[k, 0].astype(f32)
        pi = pupil[k, 1].astype(f32)
        total[0] += pr * er + pi * ei
        total[1] += pr * ei - pi * er

    sorted_back = jnp.concatenate(
        [dot(total[c].astype(bf16), gather).astype(bf16) for c in range(2)], 1
    )
    band[...] = lax.dot_general(
        chosen, sorted_back, (((0,), (0,)), ((), ())), preferred_element_type=f32
    )
    out_ref[...] = jnp.zeros_like(out_ref)
    for b in range(block_count):
        out_ref[owner_ref[b], place[b]] = band[b * blk:(b + 1) * blk, :].astype(bf16)


def add_kernel(column_ref, strips_ref, out_ref):
    led_count, slots, blk, double = strips_ref.shape
    window = double // 2
    columns = out_ref.shape[3]
    span = window + 128
    out_ref[...] = jnp.zeros_like(out_ref)

    @pl.loop(0, led_count)
    def _(led):
        base, shift = aligned(column_ref[led], span, columns)
        for s in range(slots):
            for c in range(2):
                strip = strips_ref[led, s, :, c * window:(c + 1) * window].astype(f32)
                wide = jnp.concatenate([strip, jnp.zeros((blk, 128), f32)], 1)
                out_ref[s, c, :, pl.ds(base, span)] += pltpu.roll(wide, shift, 1)


def shards(spectrum, block_owner, row_offset, column_offset, pupil_modes, amplitude):
    slots, blk, _, columns = spectrum.shape
    led_count = lax.axis_size("led")
    modes, _, w, _ = pupil_modes.shape
    m = amplitude.shape[1]
    rows = block_owner.shape[0] * blk
    left, right = dft_tables(m, w)
    perm = np.stack(deinterleave(w))
    limit = pltpu.CompilerParams(vmem_limit_bytes=50 * 1024 * 1024)
    strips_shape = jax.ShapeDtypeStruct((led_count, slots, blk, 2 * w), bf16)
    strips = pl.pallas_call(
        crop_kernel,
        out_shape=strips_shape,
        in_specs=[SMEM, VMEM],
        out_specs=VMEM,
        compiler_params=limit,
        name="crop_windows",
    )(column_offset, spectrum.transpose(2, 0, 1, 3))
    strips = lax.all_to_all(strips, "led", split_axis=0, concat_axis=0, tiled=True)
    strips = pl.pallas_call(
        gradient_kernel,
        out_shape=strips_shape,
        in_specs=[SMEM, SMEM] + [VMEM] * 6,
        out_specs=VMEM,
        scratch_shapes=[
            pltpu.VMEM((rows, 2 * w), f32),
            pltpu.VMEM((modes, 2, m, m), f32),
            pltpu.VMEM((modes, 2, w, w), bf16),
            pltpu.VMEM((m, m), f32),
            pltpu.VMEM((2, w, w), f32),
            pltpu.SMEM((led_count,), jnp.int32),
            pltpu.SMEM((block_owner.shape[0],), jnp.int32),
        ],
        compiler_params=limit,
        name="window_gradient",
    )(
        block_owner, row_offset, strips, pupil_modes, amplitude,
        jnp.asarray(left), jnp.asarray(right), jnp.asarray(perm),
    )
    strips = lax.all_to_all(strips, "led", split_axis=0, concat_axis=0, tiled=True)
    result = pl.pallas_call(
        add_kernel,
        out_shape=jax.ShapeDtypeStruct((slots, 2, blk, columns), f32),
        in_specs=[SMEM, VMEM],
        out_specs=VMEM,
        compiler_params=limit,
        name="add_strips",
    )(column_offset, strips)
    return result.transpose(0, 2, 1, 3)


def solution(mesh):
    return jax.shard_map(
        shards,
        mesh=mesh,
        in_specs=(
            P(("rep", "led"), None, None, None),
            P(),
            P(),
            P(),
            P(),
            P(("rep", "led"), None, None),
        ),
        out_specs=P(("rep", "led"), None, None, None),
        check_vma=False,
    )
```

```python
import functools
import math

import jax
import jax.numpy as jnp
import ml_dtypes
import numpy as np
from jax import lax
from jax.experimental import pallas as pl
from jax.experimental.pallas import tpu as pltpu
from jax.sharding import PartitionSpec as P

amp_eps = 0.1
f32 = jnp.float32
bf16 = jnp.bfloat16
VMEM = pl.BlockSpec(memory_space=pltpu.VMEM)
ANY = pl.BlockSpec(memory_space=pl.ANY)
SMEM = pl.BlockSpec(memory_space=pltpu.SMEM)


def dft_tables(image_side, window_side):
    half = image_side // 2
    pixel = np.arange(half, dtype=np.int64)[:, None]
    freq = np.arange(window_side, dtype=np.int64)[None, :] - window_side // 2
    phase = np.mod(pixel * freq, image_side).astype(np.float64) * (2.0 * math.pi / image_side)
    scale = 1.0 / math.sqrt(image_side)
    real = (np.cos(phase) * scale).astype(np.float32).astype(ml_dtypes.bfloat16)
    imag = (np.sin(phase) * scale).astype(np.float32).astype(ml_dtypes.bfloat16)
    left = []
    for parity in (0, 1):
        a, b = real[:, parity::2], imag[:, parity::2]
        left.append(np.block([[a, -b], [b, a]]))
    left = np.stack(left)
    right = np.ascontiguousarray(left.transpose(0, 2, 1))
    return left, right


def deinterleave(side):
    order = np.concatenate([np.arange(0, side, 2), np.arange(1, side, 2)])
    perm = (np.arange(side)[:, None] == order[None, :]).astype(ml_dtypes.bfloat16)
    return perm, np.ascontiguousarray(perm.T)


def dot(a, b):
    return jnp.dot(a, b, preferred_element_type=f32)


def aligned(column, span, columns):
    base = jnp.minimum((column // 128) * 128, columns - span)
    return pl.multiple_of(base, 128), column - base


def greet(led_count, me):
    barrier = pltpu.get_barrier_semaphore()

    @pl.loop(1, led_count)
    def _(step):
        pl.semaphore_signal(
            barrier, inc=1, device_id={"led": lax.rem(me + step, led_count)},
            device_id_type=pl.DeviceIdType.MESH,
        )

    pl.semaphore_wait(barrier, led_count - 1)


def strip_copy(step, me, led_count, source, landing, send_sem, recv_sem):
    dest = lax.rem(me + step, led_count)
    return pltpu.make_async_remote_copy(
        src_ref=source.at[dest],
        dst_ref=landing.at[me],
        send_sem=send_sem.at[step],
        recv_sem=recv_sem.at[step],
        device_id={"led": dest},
        device_id_type=pl.DeviceIdType.MESH,
    )


def far_first(turn, led_count):
    return 1 + lax.rem(turn + led_count // 2 - 1, led_count - 1)


def crop_kernel(column_ref, spectrum_ref, out_ref):
    led_count, slots, _, double = out_ref.shape
    window = double // 2
    columns = spectrum_ref.shape[3]
    span = window + 128

    @pl.loop(0, led_count)
    def _(led):
        base, shift = aligned(column_ref[led], span, columns)
        for s in range(slots):
            for c in range(2):
                wide = spectrum_ref[c, s, :, pl.ds(base, span)].astype(f32)
                wide = pltpu.roll(wide, span - shift, 1)
                out_ref[led, s, :, c * window:(c + 1) * window] = wide[:, :window].astype(bf16)


def send_kernel(
    strips, pupil_ref, perm_ref, landing, sorted_ref, send_sem, recv_sem, own_sem,
):
    led_count = strips.shape[0]
    me = lax.axis_index("led")
    own = pltpu.make_async_copy(strips.at[me], landing.at[me], own_sem)
    own.start()
    greet(led_count, me)

    @pl.loop(0, led_count - 1)
    def _(turn):
        step = far_first(turn, led_count)
        strip_copy(step, me, led_count, strips, landing, send_sem, recv_sem).start()

    @pl.loop(0, pupil_ref.shape[0])
    def _(k):
        for c in range(2):
            mixed = dot(perm_ref[1], pupil_ref[k, c]).astype(bf16)
            sorted_ref[k, c] = dot(mixed, perm_ref[0]).astype(bf16)

    own.wait()

    @pl.loop(1, led_count)
    def _(step):
        strip_copy(step, me, led_count, strips, landing, send_sem, recv_sem).wait()


def return_kernel(strips, landing, send_sem, recv_sem, own_sem):
    led_count = strips.shape[0]
    me = lax.axis_index("led")
    own = pltpu.make_async_copy(strips.at[me], landing.at[me], own_sem)
    own.start()
    greet(led_count, me)

    @pl.loop(0, led_count - 1)
    def _(turn):
        step = far_first(turn, led_count)
        strip_copy(step, me, led_count, strips, landing, send_sem, recv_sem).start()

    own.wait()

    @pl.loop(1, led_count)
    def _(step):
        strip_copy(step, me, led_count, strips, landing, send_sem, recv_sem).wait()


def gradient_kernel(
    owner_ref, row_ref, strips_ref, pupil_ref, amp_ref, left_ref, right_ref, perm_ref, out_ref,
    band, psi, weight, total, used, place,
):
    led_count, slots, blk, double = strips_ref.shape
    modes, _, w, _ = pupil_ref.shape
    m = amp_ref.shape[1]
    half, h = m // 2, w // 2
    block_count = owner_ref.shape[0]
    rows = block_count * blk
    my_row = row_ref[lax.axis_index("led")]

    for n in range(led_count):
        used[n] = 0
    for b in range(block_count):
        owner = owner_ref[b]
        rank = used[owner]
        used[owner] = rank + 1
        place[b] = rank
        band[b * blk:(b + 1) * blk, :] = strips_ref[owner, rank].astype(f32)

    line = lax.broadcasted_iota(jnp.int32, (w, rows), 0)
    natural = jnp.where(line < h, 2 * line, 2 * line - w + 1)
    chosen = lax.broadcasted_iota(jnp.int32, (w, rows), 1) == natural + my_row
    chosen = jnp.where(chosen, 1.0, 0.0).astype(bf16)
    spread, gather = perm_ref[0], perm_ref[1]
    picked = dot(chosen, band[...].astype(bf16)).astype(bf16)
    xr = dot(picked[:, :w], spread)
    xi = dot(picked[:, w:], spread)

    weight[...] = jnp.zeros_like(weight)

    @pl.loop(0, modes)
    def _(k):
        pr = pupil_ref[k, 0].astype(f32)
        pi = pupil_ref[k, 1].astype(f32)
        yr = (xr * pr - xi * pi).astype(bf16)
        yi = (xr * pi + xi * pr).astype(bf16)
        even = dot(jnp.concatenate([yr[:, :h], yi[:, :h]], 1), right_ref[0])
        odd = dot(jnp.concatenate([yr[:, h:], yi[:, h:]], 1), right_ref[1])
        low = (even + odd).astype(bf16)
        high = (even - odd).astype(bf16)

        def stacked(lo, hi):
            return jnp.concatenate(
                [
                    jnp.concatenate([low[lo:hi, :half], high[lo:hi, :half]], 1),
                    jnp.concatenate([low[lo:hi, half:], high[lo:hi, half:]], 1),
                ],
                0,
            )

        even = dot(left_ref[0], stacked(0, h))
        odd = dot(left_ref[1], stacked(h, w))
        top = even + odd
        bottom = even - odd
        psi[k, 0] = top
        psi[k, 1] = bottom
        weight[:half] += top[:half] * top[:half] + top[half:] * top[half:]
        weight[half:] += bottom[:half] * bottom[:half] + bottom[half:] * bottom[half:]

    modulus = jnp.sqrt(weight[...] + amp_eps)
    weight[...] = (modulus - amp_ref[0]) / modulus
    total[...] = jnp.zeros_like(total)

    @pl.loop(0, modes)
    def _(k):
        wt = weight[:half]
        wb = weight[half:]
        sums, differences = [], []
        for part in (slice(0, half), slice(half, m)):
            top = psi[k, 0, part] * wt
            bottom = psi[k, 1, part] * wb
            sums.append((top + bottom).astype(bf16))
            differences.append((top - bottom).astype(bf16))
        even = dot(right_ref[0], jnp.concatenate(sums, 0))
        odd = dot(right_ref[1], jnp.concatenate(differences, 0))
        hr = jnp.concatenate([even[:h], odd[:h]], 0)
        hi = jnp.concatenate([even[h:], odd[h:]], 0)
        plus = jnp.concatenate([hr[:, :half] + hr[:, half:], hi[:, :half] + hi[:, half:]], 1)
        minus = jnp.concatenate([hr[:, :half] - hr[:, half:], hi[:, :half] - hi[:, half:]], 1)
        even = dot(plus.astype(bf16), left_ref[0])
        odd = dot(minus.astype(bf16), left_ref[1])
        er = jnp.concatenate([even[:, :h], odd[:, :h]], 1)
        ei = jnp.concatenate([even[:, h:], odd[:, h:]], 1)
        pr = pupil_ref[k, 0].astype(f32)
        pi = pupil_ref[k, 1].astype(f32)
        total[0] += pr * er + pi * ei
        total[1] += pr * ei - pi * er

    sorted_back = jnp.concatenate(
        [dot(total[c].astype(bf16), gather).astype(bf16) for c in range(2)], 1
    )
    band[...] = lax.dot_general(
        chosen, sorted_back, (((0,), (0,)), ((), ())), preferred_element_type=f32
    )
    out_ref[...] = jnp.zeros_like(out_ref)
    for b in range(block_count):
        out_ref[owner_ref[b], place[b]] = band[b * blk:(b + 1) * blk, :].astype(bf16)


def add_kernel(column_ref, strips_ref, out_ref, total):
    led_count, slots, blk, double = strips_ref.shape
    window = double // 2
    columns = out_ref.shape[3]
    span = window + 128
    total[...] = jnp.zeros_like(total)

    @pl.loop(0, led_count)
    def _(led):
        base, shift = aligned(column_ref[led], span, columns)
        for s in range(slots):
            for c in range(2):
                strip = strips_ref[led, s, :, c * window:(c + 1) * window].astype(f32)
                wide = jnp.concatenate([strip, jnp.zeros((blk, 128), f32)], 1)
                total[s, c, :, pl.ds(base, span)] += pltpu.roll(wide, shift, 1)

    for s in range(slots):
        for c in range(2):
            out_ref[s, :, c, :] = total[s, c]


def shards(spectrum, block_owner, row_offset, column_offset, pupil_modes, amplitude):
    slots, blk, _, columns = spectrum.shape
    led_count = lax.axis_size("led")
    modes, _, w, _ = pupil_modes.shape
    m = amplitude.shape[1]
    rows = block_owner.shape[0] * blk
    left, right = dft_tables(m, w)
    perm = np.stack(deinterleave(w))
    limit = functools.partial(pltpu.CompilerParams, vmem_limit_bytes=48 * 1024 * 1024)
    strips_shape = jax.ShapeDtypeStruct((led_count, slots, blk, 2 * w), bf16)
    semaphores = [
        pltpu.SemaphoreType.DMA((led_count,)),
        pltpu.SemaphoreType.DMA((led_count,)),
        pltpu.SemaphoreType.DMA,
    ]
    strips = pl.pallas_call(
        crop_kernel,
        out_shape=strips_shape,
        in_specs=[SMEM, VMEM],
        out_specs=VMEM,
        compiler_params=limit(),
        name="crop_windows",
    )(column_offset, spectrum.transpose(2, 0, 1, 3))
    strips, pupil_sorted = pl.pallas_call(
        send_kernel,
        out_shape=(strips_shape, jax.ShapeDtypeStruct(pupil_modes.shape, bf16)),
        in_specs=[ANY, VMEM, VMEM],
        out_specs=(ANY, VMEM),
        scratch_shapes=semaphores,
        compiler_params=limit(collective_id=0, has_side_effects=True),
        name="send_windows",
    )(strips, pupil_modes, jnp.asarray(perm))
    strips = pl.pallas_call(
        gradient_kernel,
        out_shape=strips_shape,
        in_specs=[SMEM, SMEM] + [VMEM] * 6,
        out_specs=VMEM,
        scratch_shapes=[
            pltpu.VMEM((rows, 2 * w), f32),
            pltpu.VMEM((modes, 2, m, m), f32),
            pltpu.VMEM((m, m), f32),
            pltpu.VMEM((2, w, w), f32),
            pltpu.SMEM((led_count,), jnp.int32),
            pltpu.SMEM((block_owner.shape[0],), jnp.int32),
        ],
        compiler_params=limit(),
        name="window_gradient",
    )(
        block_owner, row_offset, strips, pupil_sorted, amplitude,
        jnp.asarray(left), jnp.asarray(right), jnp.asarray(perm),
    )
    strips = pl.pallas_call(
        return_kernel,
        out_shape=strips_shape,
        in_specs=[ANY],
        out_specs=ANY,
        scratch_shapes=semaphores,
        compiler_params=limit(collective_id=1, has_side_effects=True),
        name="return_strips",
    )(strips)
    return pl.pallas_call(
        add_kernel,
        out_shape=jax.ShapeDtypeStruct((slots, blk, 2, columns), f32),
        in_specs=[SMEM, VMEM],
        out_specs=VMEM,
        scratch_shapes=[pltpu.VMEM((slots, 2, blk, columns), f32)],
        compiler_params=limit(),
        name="add_strips",
    )(column_offset, strips)


def solution(mesh):
    return jax.shard_map(
        shards,
        mesh=mesh,
        in_specs=(
            P(("rep", "led"), None, None, None),
            P(),
            P(),
            P(),
            P(),
            P(("rep", "led"), None, None),
        ),
        out_specs=P(("rep", "led"), None, None, None),
        check_vma=False,
    )
```

```python
import functools
import math

import jax
import jax.numpy as jnp
import ml_dtypes
import numpy as np
from jax import lax
from jax.experimental import pallas as pl
from jax.experimental.pallas import tpu as pltpu
from jax.sharding import PartitionSpec as P

amp_eps = 0.1
f32 = jnp.float32
bf16 = jnp.bfloat16
VMEM = pl.BlockSpec(memory_space=pltpu.VMEM)
ANY = pl.BlockSpec(memory_space=pl.ANY)
SMEM = pl.BlockSpec(memory_space=pltpu.SMEM)


def dft_tables(image_side, window_side):
    half = image_side // 2
    pixel = np.arange(half, dtype=np.int64)[:, None]
    freq = np.arange(window_side, dtype=np.int64)[None, :] - window_side // 2
    phase = np.mod(pixel * freq, image_side).astype(np.float64) * (2.0 * math.pi / image_side)
    scale = 1.0 / math.sqrt(image_side)
    real = (np.cos(phase) * scale).astype(np.float32).astype(ml_dtypes.bfloat16)
    imag = (np.sin(phase) * scale).astype(np.float32).astype(ml_dtypes.bfloat16)
    left = []
    for parity in (0, 1):
        a, b = real[:, parity::2], imag[:, parity::2]
        left.append(np.block([[a, -b], [b, a]]))
    left = np.stack(left)
    right = np.ascontiguousarray(left.transpose(0, 2, 1))
    return left, right


def deinterleave(side):
    order = np.concatenate([np.arange(0, side, 2), np.arange(1, side, 2)])
    perm = (np.arange(side)[:, None] == order[None, :]).astype(ml_dtypes.bfloat16)
    return perm, np.ascontiguousarray(perm.T)


def dot(a, b):
    return jnp.dot(a, b, preferred_element_type=f32)


def aligned(column, span, columns):
    base = jnp.minimum((column // 128) * 128, columns - span)
    return pl.multiple_of(base, 128), column - base


def greet(led_count, me):
    barrier = pltpu.get_barrier_semaphore()

    @pl.loop(1, led_count)
    def _(step):
        pl.semaphore_signal(
            barrier, inc=1, device_id={"led": lax.rem(me + step, led_count)},
            device_id_type=pl.DeviceIdType.MESH,
        )

    pl.semaphore_wait(barrier, led_count - 1)


def strip_copy(step, me, led_count, source, landing, send_sem, recv_sem):
    dest = lax.rem(me + step, led_count)
    return pltpu.make_async_remote_copy(
        src_ref=source.at[dest],
        dst_ref=landing.at[me],
        send_sem=send_sem.at[step],
        recv_sem=recv_sem.at[step],
        device_id={"led": dest},
        device_id_type=pl.DeviceIdType.MESH,
    )


def far_first(turn, led_count):
    return 1 + lax.rem(turn + led_count // 2 - 1, led_count - 1)


def crop_kernel(owner_ref, row_ref, column_ref, spectrum_ref, out_ref, line_ref, used):
    led_count, depth, double = out_ref.shape
    _, slots, blk, columns = spectrum_ref.shape
    window = double // 2
    span = window + 128
    if depth > slots * blk:
        out_ref[...] = jnp.zeros_like(out_ref)

    @pl.loop(0, led_count)
    def _(led):
        base, shift = aligned(column_ref[led], span, columns)
        for s in range(slots):
            for c in range(2):
                wide = spectrum_ref[c, s, :, pl.ds(base, span)].astype(f32)
                wide = pltpu.roll(wide, span - shift, 1)
                out_ref[led, s * blk:(s + 1) * blk, c * window:(c + 1) * window] = (
                    wide[:, :window].astype(bf16)
                )

    my_row = row_ref[lax.axis_index("led")]
    for n in range(led_count):
        used[n] = 0
    place = lax.broadcasted_iota(jnp.int32, line_ref.shape, 1)
    line = jnp.full(line_ref.shape, -1, jnp.int32)
    for b in range(owner_ref.shape[0]):
        owner = owner_ref[b]
        rank = used[owner]
        used[owner] = rank + 1
        inside = place - (owner * depth + rank * blk)
        line = jnp.where((inside >= 0) & (inside < blk), inside + (b * blk - my_row), line)
    line_ref[...] = line


def gradient_kernel(
    line_ref, strips, pupil_ref, amp_ref, left_ref, right_ref, perm_ref, returned,
    arrived, leaving, chosen, chosen_back, psi, pupil, weight, total,
    send_sem, recv_sem, back_send_sem, back_recv_sem, own_sem,
):
    led_count, depth, double = strips.shape
    modes, _, w, _ = pupil_ref.shape
    m = amp_ref.shape[1]
    half, h = m // 2, w // 2
    rows = led_count * depth
    me = lax.axis_index("led")

    def exchange(source, landing, sends, recvs, beside):
        own = pltpu.make_async_copy(source.at[me], landing.at[me], own_sem)
        own.start()

        @pl.loop(0, led_count - 1)
        def _(turn):
            step = far_first(turn, led_count)
            strip_copy(step, me, led_count, source, landing, sends, recvs).start()

        beside()
        own.wait()

        @pl.loop(1, led_count)
        def _(step):
            strip_copy(step, me, led_count, source, landing, sends, recvs).wait()

    spread, gather = perm_ref[0], perm_ref[1]

    def prepare():
        place = lax.broadcasted_iota(jnp.int32, (w, rows), 0)
        natural = jnp.where(place < h, 2 * place, 2 * place - w + 1)
        picks = jnp.where(line_ref[0:1] == natural, 1.0, 0.0)
        chosen[...] = picks.astype(bf16)
        chosen_back[...] = picks.T.astype(bf16)

        @pl.loop(0, modes)
        def _(k):
            for c in range(2):
                mixed = dot(perm_ref[1], pupil_ref[k, c]).astype(bf16)
                pupil[k, c] = dot(mixed, perm_ref[0])

        weight[...] = jnp.zeros_like(weight)
        total[...] = jnp.zeros_like(total)

    greet(led_count, me)
    exchange(strips, arrived, send_sem, recv_sem, prepare)

    picked = dot(chosen[...], arrived[...].reshape(rows, double)).astype(bf16)
    xr = dot(picked[:, :w], spread)
    xi = dot(picked[:, w:], spread)

    @pl.loop(0, modes)
    def _(k):
        pr = pupil[k, 0]
        pi = pupil[k, 1]
        yr = (xr * pr - xi * pi).astype(bf16)
        yi = (xr * pi + xi * pr).astype(bf16)
        even = dot(jnp.concatenate([yr[:, :h], yi[:, :h]], 1), right_ref[0])
        odd = dot(jnp.concatenate([yr[:, h:], yi[:, h:]], 1), right_ref[1])
        low = (even + odd).astype(bf16)
        high = (even - odd).astype(bf16)

        def stacked(lo, hi):
            return jnp.concatenate(
                [
                    jnp.concatenate([low[lo:hi, :half], high[lo:hi, :half]], 1),
                    jnp.concatenate([low[lo:hi, half:], high[lo:hi, half:]], 1),
                ],
                0,
            )

        even = dot(left_ref[0], stacked(0, h))
        odd = dot(left_ref[1], stacked(h, w))
        top = even + odd
        bottom = even - odd
        psi[k, 0] = top
        psi[k, 1] = bottom
        weight[:half] += top[:half] * top[:half] + top[half:] * top[half:]
        weight[half:] += bottom[:half] * bottom[:half] + bottom[half:] * bottom[half:]

    modulus = jnp.sqrt(weight[...] + amp_eps)
    weight[...] = (modulus - amp_ref[0]) / modulus

    @pl.loop(0, modes)
    def _(k):
        wt = weight[:half]
        wb = weight[half:]
        sums, differences = [], []
        for part in (slice(0, half), slice(half, m)):
            top = psi[k, 0, part] * wt
            bottom = psi[k, 1, part] * wb
            sums.append((top + bottom).astype(bf16))
            differences.append((top - bottom).astype(bf16))
        even = dot(right_ref[0], jnp.concatenate(sums, 0))
        odd = dot(right_ref[1], jnp.concatenate(differences, 0))
        hr = jnp.concatenate([even[:h], odd[:h]], 0)
        hi = jnp.concatenate([even[h:], odd[h:]], 0)
        plus = jnp.concatenate([hr[:, :half] + hr[:, half:], hi[:, :half] + hi[:, half:]], 1)
        minus = jnp.concatenate([hr[:, :half] - hr[:, half:], hi[:, :half] - hi[:, half:]], 1)
        even = dot(plus.astype(bf16), left_ref[0])
        odd = dot(minus.astype(bf16), left_ref[1])
        er = jnp.concatenate([even[:, :h], odd[:, :h]], 1)
        ei = jnp.concatenate([even[:, h:], odd[:, h:]], 1)
        pr = pupil[k, 0]
        pi = pupil[k, 1]
        total[0] += pr * er + pi * ei
        total[1] += pr * ei - pi * er

    sorted_back = jnp.concatenate(
        [dot(total[c].astype(bf16), gather).astype(bf16) for c in range(2)], 1
    )
    leaving[...] = dot(chosen_back[...], sorted_back).astype(bf16).reshape(leaving.shape)
    exchange(leaving, returned, back_send_sem, back_recv_sem, lambda: None)


def add_kernel(column_ref, strips_ref, out_ref, total):
    led_count, _, double = strips_ref.shape
    slots, blk, _, columns = out_ref.shape
    window = double // 2
    span = window + 128
    total[...] = jnp.zeros_like(total)

    @pl.loop(0, led_count)
    def _(led):
        base, shift = aligned(column_ref[led], span, columns)
        for s in range(slots):
            for c in range(2):
                strip = strips_ref[led, s * blk:(s + 1) * blk, c * window:(c + 1) * window]
                strip = strip.astype(f32)
                wide = jnp.concatenate([strip, jnp.zeros((blk, 128), f32)], 1)
                total[s, c, :, pl.ds(base, span)] += pltpu.roll(wide, shift, 1)

    for s in range(slots):
        for c in range(2):
            out_ref[s, :, c, :] = total[s, c]


def shards(spectrum, block_owner, row_offset, column_offset, pupil_modes, amplitude):
    slots, blk, _, columns = spectrum.shape
    led_count = lax.axis_size("led")
    modes, _, w, _ = pupil_modes.shape
    m = amplitude.shape[1]
    depth = -(-slots * blk // 16) * 16
    rows = led_count * depth
    left, right = dft_tables(m, w)
    perm = np.stack(deinterleave(w))
    limit = functools.partial(pltpu.CompilerParams, vmem_limit_bytes=48 * 1024 * 1024)
    strips_shape = jax.ShapeDtypeStruct((led_count, depth, 2 * w), bf16)
    strips, line = pl.pallas_call(
        crop_kernel,
        out_shape=(strips_shape, jax.ShapeDtypeStruct((8, rows), jnp.int32)),
        in_specs=[SMEM, SMEM, SMEM, VMEM],
        out_specs=(VMEM, VMEM),
        scratch_shapes=[pltpu.SMEM((led_count,), jnp.int32)],
        compiler_params=limit(),
        name="crop_windows",
    )(block_owner, row_offset, column_offset, spectrum.transpose(2, 0, 1, 3))
    strips = pl.pallas_call(
        gradient_kernel,
        out_shape=strips_shape,
        in_specs=[VMEM, ANY] + [VMEM] * 5,
        out_specs=ANY,
        scratch_shapes=[
            pltpu.VMEM(strips_shape.shape, bf16),
            pltpu.VMEM(strips_shape.shape, bf16),
            pltpu.VMEM((w, rows), bf16),
            pltpu.VMEM((rows, w), bf16),
            pltpu.VMEM((modes, 2, m, m), f32),
            pltpu.VMEM((modes, 2, w, w), f32),
            pltpu.VMEM((m, m), f32),
            pltpu.VMEM((2, w, w), f32),
            pltpu.SemaphoreType.DMA((led_count,)),
            pltpu.SemaphoreType.DMA((led_count,)),
            pltpu.SemaphoreType.DMA((led_count,)),
            pltpu.SemaphoreType.DMA((led_count,)),
            pltpu.SemaphoreType.DMA,
        ],
        compiler_params=limit(collective_id=0, has_side_effects=True),
        name="window_gradient",
    )(
        line, strips, pupil_modes, amplitude,
        jnp.asarray(left), jnp.asarray(right), jnp.asarray(perm),
    )
    return pl.pallas_call(
        add_kernel,
        out_shape=jax.ShapeDtypeStruct((slots, blk, 2, columns), f32),
        in_specs=[SMEM, VMEM],
        out_specs=VMEM,
        scratch_shapes=[pltpu.VMEM((slots, 2, blk, columns), f32)],
        compiler_params=limit(),
        name="add_strips",
    )(column_offset, strips)


def solution(mesh):
    return jax.shard_map(
        shards,
        mesh=mesh,
        in_specs=(
            P(("rep", "led"), None, None, None),
            P(),
            P(),
            P(),
            P(),
            P(("rep", "led"), None, None),
        ),
        out_specs=P(("rep", "led"), None, None, None),
        check_vma=False,
    )
```

```python
import functools
import math

import jax
import jax.numpy as jnp
import ml_dtypes
import numpy as np
from jax import lax
from jax.experimental import pallas as pl
from jax.experimental.pallas import tpu as pltpu
from jax.sharding import PartitionSpec as P

amp_eps = 0.1
f32 = jnp.float32
bf16 = jnp.bfloat16
VMEM = pl.BlockSpec(memory_space=pltpu.VMEM)
ANY = pl.BlockSpec(memory_space=pl.ANY)
SMEM = pl.BlockSpec(memory_space=pltpu.SMEM)


def dft_tables(image_side, window_side):
    half = image_side // 2
    pixel = np.arange(half, dtype=np.int64)[:, None]
    freq = np.arange(window_side, dtype=np.int64)[None, :] - window_side // 2
    phase = np.mod(pixel * freq, image_side).astype(np.float64) * (2.0 * math.pi / image_side)
    scale = 1.0 / math.sqrt(image_side)
    real = (np.cos(phase) * scale).astype(np.float32).astype(ml_dtypes.bfloat16)
    imag = (np.sin(phase) * scale).astype(np.float32).astype(ml_dtypes.bfloat16)
    left = []
    for parity in (0, 1):
        a, b = real[:, parity::2], imag[:, parity::2]
        left.append(np.block([[a, -b], [b, a]]))
    left = np.stack(left)
    right = np.ascontiguousarray(left.transpose(0, 2, 1))
    return left, right


def deinterleave(side):
    order = np.concatenate([np.arange(0, side, 2), np.arange(1, side, 2)])
    perm = (np.arange(side)[:, None] == order[None, :]).astype(ml_dtypes.bfloat16)
    return perm, np.ascontiguousarray(perm.T)


def dot(a, b):
    return jnp.dot(a, b, preferred_element_type=f32)


def aligned(column, span, columns):
    base = jnp.minimum((column // 128) * 128, columns - span)
    return pl.multiple_of(base, 128), column - base


def greet(led_count, me):
    barrier = pltpu.get_barrier_semaphore()

    @pl.loop(1, led_count)
    def _(step):
        pl.semaphore_signal(
            barrier, inc=1, device_id={"led": lax.rem(me + step, led_count)},
            device_id_type=pl.DeviceIdType.MESH,
        )

    pl.semaphore_wait(barrier, led_count - 1)


def strip_copy(step, me, led_count, source, landing, send_sem, recv_sem):
    dest = lax.rem(me + step, led_count)
    return pltpu.make_async_remote_copy(
        src_ref=source.at[dest],
        dst_ref=landing.at[me],
        send_sem=send_sem.at[step],
        recv_sem=recv_sem.at[step],
        device_id={"led": dest},
        device_id_type=pl.DeviceIdType.MESH,
    )


def far_first(turn, led_count):
    return 1 + lax.rem(turn + led_count // 2 - 1, led_count - 1)


def crop_kernel(
    slots, owner_ref, row_ref, column_ref, spectrum_ref, out_ref, line_ref, used,
):
    led_count, depth, double = out_ref.shape
    rows, columns = spectrum_ref.shape
    height = rows // 2
    blk = height // slots
    window = double // 2
    span = window + 128
    if depth > height:
        out_ref[...] = jnp.zeros_like(out_ref)

    @pl.loop(0, led_count, unroll=4)
    def _(led):
        base, shift = aligned(column_ref[led], span, columns)
        wide = pltpu.roll(spectrum_ref[:, pl.ds(base, span)].astype(f32), span - shift, 1)
        wide = jnp.concatenate([wide[:height, :window], wide[height:, :window]], 1)
        out_ref[led, :height, :] = wide.astype(bf16)

    my_row = row_ref[lax.axis_index("led")]
    for n in range(led_count):
        used[n] = 0
    place = lax.broadcasted_iota(jnp.int32, line_ref.shape, 1)
    line = jnp.full(line_ref.shape, -1, jnp.int32)
    for b in range(owner_ref.shape[0]):
        owner = owner_ref[b]
        rank = used[owner]
        used[owner] = rank + 1
        inside = place - (owner * depth + rank * blk)
        line = jnp.where((inside >= 0) & (inside < blk), inside + (b * blk - my_row), line)
    line_ref[...] = line


def gradient_kernel(
    line_ref, strips, pupil_hbm, amp_hbm, left_hbm, right_hbm, perm_hbm, returned,
    pupil_ref, amp_ref, left_ref, right_ref, perm_ref, arrived, leaving, chosen, chosen_back, psi, pupil, weight, total,
    send_sem, recv_sem, back_send_sem, back_recv_sem, own_sem, load_sem,
):
    led_count, depth, double = strips.shape
    modes, _, w, _ = pupil_ref.shape
    m = amp_ref.shape[1]
    half, h = m // 2, w // 2
    rows = led_count * depth
    me = lax.axis_index("led")

    def exchange(source, landing, sends, recvs, beside):
        own = pltpu.make_async_copy(source.at[me], landing.at[me], own_sem)
        own.start()

        @pl.loop(0, led_count - 1)
        def _(turn):
            step = far_first(turn, led_count)
            strip_copy(step, me, led_count, source, landing, sends, recvs).start()

        beside()
        own.wait()

        @pl.loop(1, led_count)
        def _(step):
            strip_copy(step, me, led_count, source, landing, sends, recvs).wait()

    loads = [
        pltpu.make_async_copy(source, target, load_sem.at[n])
        for n, (source, target) in enumerate(
            [
                (perm_hbm, perm_ref), (pupil_hbm, pupil_ref), (amp_hbm, amp_ref),
                (left_hbm, left_ref), (right_hbm, right_ref),
            ]
        )
    ]

    def prepare():
        for load in loads:
            load.start()
        place = lax.broadcasted_iota(jnp.int32, (w, rows), 0)
        natural = jnp.where(place < h, 2 * place, 2 * place - w + 1)
        picks = jnp.where(line_ref[0:1] == natural, 1.0, 0.0)
        chosen[...] = picks.astype(bf16)
        chosen_back[...] = picks.T.astype(bf16)

        for load in loads:
            load.wait()

        @pl.loop(0, modes)
        def _(k):
            for c in range(2):
                mixed = dot(perm_ref[1], pupil_ref[k, c]).astype(bf16)
                pupil[k, c] = dot(mixed, perm_ref[0])

        weight[...] = jnp.zeros_like(weight)
        total[...] = jnp.zeros_like(total)

    greet(led_count, me)
    exchange(strips, arrived, send_sem, recv_sem, prepare)

    spread, gather = perm_ref[0], perm_ref[1]
    picked = dot(chosen[...], arrived[...].reshape(rows, double)).astype(bf16)
    xr = dot(picked[:, :w], spread)
    xi = dot(picked[:, w:], spread)

    @pl.loop(0, modes, unroll=modes)
    def _(k):
        pr = pupil[k, 0]
        pi = pupil[k, 1]
        yr = (xr * pr - xi * pi).astype(bf16)
        yi = (xr * pi + xi * pr).astype(bf16)
        even = dot(jnp.concatenate([yr[:, :h], yi[:, :h]], 1), right_ref[0])
        odd = dot(jnp.concatenate([yr[:, h:], yi[:, h:]], 1), right_ref[1])
        low = (even + odd).astype(bf16)
        high = (even - odd).astype(bf16)

        def stacked(lo, hi):
            return jnp.concatenate(
                [
                    jnp.concatenate([low[lo:hi, :half], high[lo:hi, :half]], 1),
                    jnp.concatenate([low[lo:hi, half:], high[lo:hi, half:]], 1),
                ],
                0,
            )

        even = dot(left_ref[0], stacked(0, h))
        odd = dot(left_ref[1], stacked(h, w))
        top = even + odd
        bottom = even - odd
        psi[k, 0] = top
        psi[k, 1] = bottom
        weight[:half] += top[:half] * top[:half] + top[half:] * top[half:]
        weight[half:] += bottom[:half] * bottom[:half] + bottom[half:] * bottom[half:]

    modulus = jnp.sqrt(weight[...] + amp_eps)
    weight[...] = (modulus - amp_ref[0]) / modulus

    @pl.loop(0, modes, unroll=modes)
    def _(k):
        wt = weight[:half]
        wb = weight[half:]
        sums, differences = [], []
        for part in (slice(0, half), slice(half, m)):
            top = psi[k, 0, part] * wt
            bottom = psi[k, 1, part] * wb
            sums.append((top + bottom).astype(bf16))
            differences.append((top - bottom).astype(bf16))
        even = dot(right_ref[0], jnp.concatenate(sums, 0))
        odd = dot(right_ref[1], jnp.concatenate(differences, 0))
        hr = jnp.concatenate([even[:h], odd[:h]], 0)
        hi = jnp.concatenate([even[h:], odd[h:]], 0)
        plus = jnp.concatenate([hr[:, :half] + hr[:, half:], hi[:, :half] + hi[:, half:]], 1)
        minus = jnp.concatenate([hr[:, :half] - hr[:, half:], hi[:, :half] - hi[:, half:]], 1)
        even = dot(plus.astype(bf16), left_ref[0])
        odd = dot(minus.astype(bf16), left_ref[1])
        er = jnp.concatenate([even[:, :h], odd[:, :h]], 1)
        ei = jnp.concatenate([even[:, h:], odd[:, h:]], 1)
        pr = pupil[k, 0]
        pi = pupil[k, 1]
        total[0] += pr * er + pi * ei
        total[1] += pr * ei - pi * er

    sorted_back = jnp.concatenate(
        [dot(total[c].astype(bf16), gather).astype(bf16) for c in range(2)], 1
    )
    leaving[...] = dot(chosen_back[...], sorted_back).astype(bf16).reshape(leaving.shape)
    exchange(leaving, returned, back_send_sem, back_recv_sem, lambda: None)


def add_kernel(column_ref, strips_ref, out_hbm, total, out_ref, out_sem):
    led_count, depth, double = strips_ref.shape
    slots, blk, _, columns = out_ref.shape
    window = double // 2
    span = window + 128
    total[...] = jnp.zeros_like(total)

    @pl.loop(0, led_count, unroll=4)
    def _(led):
        base, shift = aligned(column_ref[led], span, columns)
        strip = strips_ref[led].astype(f32)
        strip = jnp.concatenate([strip[:, :window], strip[:, window:]], 0)
        wide = jnp.concatenate([strip, jnp.zeros((2 * depth, 128), f32)], 1)
        total[:, pl.ds(base, span)] += pltpu.roll(wide, shift, 1)

    copies = []
    for s in range(slots):
        for c in range(2):
            first = c * depth + s * blk
            out_ref[s, :, c, :] = total[first:first + blk, :]
        copies.append(pltpu.make_async_copy(out_ref.at[s], out_hbm.at[s], out_sem.at[s]))
        copies[-1].start()
    for copy in copies:
        copy.wait()


def shards(spectrum, block_owner, row_offset, column_offset, pupil_modes, amplitude):
    slots, blk, _, columns = spectrum.shape
    led_count = lax.axis_size("led")
    modes, _, w, _ = pupil_modes.shape
    m = amplitude.shape[1]
    depth = -(-slots * blk // 16) * 16
    rows = led_count * depth
    left, right = dft_tables(m, w)
    perm = np.stack(deinterleave(w))
    limit = functools.partial(pltpu.CompilerParams, vmem_limit_bytes=60 * 1024 * 1024)
    strips_shape = jax.ShapeDtypeStruct((led_count, depth, 2 * w), bf16)
    strips, line = pl.pallas_call(
        functools.partial(crop_kernel, slots),
        out_shape=(strips_shape, jax.ShapeDtypeStruct((8, rows), jnp.int32)),
        in_specs=[SMEM, SMEM, SMEM, VMEM],
        out_specs=(VMEM, VMEM),
        scratch_shapes=[pltpu.SMEM((led_count,), jnp.int32)],
        compiler_params=pltpu.CompilerParams(vmem_limit_bytes=48 * 1024 * 1024),
        name="crop_windows",
    )(block_owner, row_offset, column_offset, spectrum.transpose(2, 0, 1, 3).reshape(2 * slots * blk, columns))
    strips = pl.pallas_call(
        gradient_kernel,
        out_shape=strips_shape,
        in_specs=[VMEM] + [ANY] * 6,
        out_specs=ANY,
        scratch_shapes=[
            pltpu.VMEM(pupil_modes.shape, bf16),
            pltpu.VMEM(amplitude.shape, f32),
            pltpu.VMEM(left.shape, bf16),
            pltpu.VMEM(right.shape, bf16),
            pltpu.VMEM(perm.shape, bf16),
            pltpu.VMEM(strips_shape.shape, bf16),
            pltpu.VMEM(strips_shape.shape, bf16),
            pltpu.VMEM((w, rows), bf16),
            pltpu.VMEM((rows, w), bf16),
            pltpu.VMEM((modes, 2, m, m), f32),
            pltpu.VMEM((modes, 2, w, w), f32),
            pltpu.VMEM((m, m), f32),
            pltpu.VMEM((2, w, w), f32),
            pltpu.SemaphoreType.DMA((led_count,)),
            pltpu.SemaphoreType.DMA((led_count,)),
            pltpu.SemaphoreType.DMA((led_count,)),
            pltpu.SemaphoreType.DMA((led_count,)),
            pltpu.SemaphoreType.DMA,
            pltpu.SemaphoreType.DMA((5,)),
        ],
        compiler_params=pltpu.CompilerParams(
            collective_id=0, has_side_effects=True, vmem_limit_bytes=60 * 1024 * 1024
        ),
        name="window_gradient",
    )(
        line, strips, pupil_modes, amplitude,
        jnp.asarray(left), jnp.asarray(right), jnp.asarray(perm),
    )
    return pl.pallas_call(
        add_kernel,
        out_shape=jax.ShapeDtypeStruct((slots, blk, 2, columns), f32),
        in_specs=[SMEM, VMEM],
        out_specs=ANY,
        scratch_shapes=[
            pltpu.VMEM((2 * depth, columns), f32),
            pltpu.VMEM((slots, blk, 2, columns), f32),
            pltpu.SemaphoreType.DMA((slots,)),
        ],
        compiler_params=limit(),
        name="add_strips",
    )(column_offset, strips)


def solution(mesh):
    return jax.shard_map(
        shards,
        mesh=mesh,
        in_specs=(
            P(("rep", "led"), None, None, None),
            P(),
            P(),
            P(),
            P(),
            P(("rep", "led"), None, None),
        ),
        out_specs=P(("rep", "led"), None, None, None),
        check_vma=False,
    )
```
